512 devices in a mesh: row: 64 (over x, y, z_hi), col: 8 (over z_lo, core).
Axes of the slice: x: 4, y: 4, z: 16 (z_hi: 4, z_lo: 4; z = z_hi * 4 + z_lo), core: 2. Of those that a mesh axis runs over, the one named last changes fastest.
Arguments:
- tokens: bfloat16 [320, 12288], P('row'), may hold values from -6 to 6
- weight: bfloat16 [12288, 24576], P('row', 'col'), may hold values from -0.0546875 to 0.0546875
- bias: float32 [24576], P('col'), may hold values from -5 to 5
- grad_out: bfloat16 [320, 24576], P('row', 'col'), may hold values from -6 to 6
Outputs:
- activation: bfloat16 [320, 24576], P('row', 'col')
- input_grad: bfloat16 [320, 12288], P('row')
- weight_grad: bfloat16 [12288, 24576], P('row', 'col')
- bias_grad: float32 [24576], P('col')
The draws below stay inside these ranges and needn't reach their ends.
All inputs are finite; a program needn't handle non-finite values.
Results may differ from the reference program's by a relative error of at most 0.019.
Values may be sent and summed in bfloat16 or wider, within the bound.
No kernel may reach another device: no remote copies, remote signals or barrier semaphores. Data moves between devices by JAX's collectives and lax.ppermute only.
A program may use at most 64 MiB of HBM per device.

```python
import math
import jax
import jax.numpy as jnp
from jax import lax

D = 12288
HIDDEN_SIZE = 24576
TOKENS = 320


def level_of(key, shape, cuts, least, top_value):
    gain = 1.0
    for dim, shards_of in cuts:
        heights = jax.random.uniform(jax.random.fold_in(jax.random.fold_in(key, 6), dim), (shards_of,), jnp.float32, least / len(cuts), top_value / len(cuts))
        gain = gain * jnp.repeat(jnp.exp(heights), shape[dim] // shards_of).reshape((-1,) + (1,) * (len(shape) - 1 - dim))
    return gain


def normal_values(own_key, extent, spread, limit, cuts=(), kind=jnp.bfloat16):
    values = spread * jax.random.normal(own_key, extent, jnp.float32)
    if cuts:
        values = values * level_of(own_key, extent, cuts, -0.22, 0.18)
    return jnp.clip(values, -limit, limit).astype(kind)


def setup_inputs(seed: int = 0) -> dict:
    key_of = jax.random.split(jax.random.key(seed), 5)
    tokens = normal_values(key_of[0], (TOKENS, D), 1.0, 6.0, ((0, 64),))
    weight = normal_values(key_of[1], (D, HIDDEN_SIZE), D ** -0.5, 0.0546875, ((0, 64), (1, 8)))
    bias = normal_values(key_of[2], (HIDDEN_SIZE,), 1.0, 5.0, ((0, 8),), jnp.float32)
    grad_out = normal_values(key_of[3], (TOKENS, HIDDEN_SIZE), 1.0, 6.0, ((0, 64), (1, 8)))
    return dict(tokens=tokens, weight=weight, bias=bias, grad_out=grad_out)


root_coeff = math.sqrt(2.0 / math.pi)
cubic_coeff = 0.044715

def gelu_parts(pre_act):
    argument = root_coeff * (pre_act + cubic_coeff * pre_act * pre_act * pre_act)
    tangent = jnp.tanh(argument)
    output_value = 0.5 * pre_act * (1.0 + tangent)
    derivative = 0.5 * (1.0 + tangent) + 0.5 * pre_act * (1.0 - tangent * tangent) * root_coeff * (1.0 + 3.0 * cubic_coeff * pre_act * pre_act)
    return (output_value, derivative)

def reference(tokens, weight, bias, grad_out):
    pre_act = jnp.dot(tokens, weight, preferred_element_type=jnp.float32) + bias
    output_value, derivative = gelu_parts(pre_act)
    activation = output_value.astype(jnp.bfloat16)
    grad_pre = (grad_out.astype(jnp.float32) * derivative).astype(jnp.bfloat16)
    bias_grad = lax.optimization_barrier(jnp.sum(grad_pre.astype(jnp.float32), axis=0))
    weight_grad = jnp.dot(tokens.T, grad_pre, preferred_element_type=jnp.float32).astype(jnp.bfloat16)
    input_grad = jnp.dot(grad_pre, weight.T, preferred_element_type=jnp.float32).astype(jnp.bfloat16)
    return (activation, input_grad, weight_grad, bias_grad)
```

```python
import math

import jax
import jax.numpy as jnp
from jax import lax
from jax.sharding import PartitionSpec as P

root_coeff = math.sqrt(2.0 / math.pi)
cubic_coeff = 0.044715

N_XY, N_Z, N_COL = 16, 4, 8
XY_GROUPS = [[p * N_Z + z for p in range(N_XY)] for z in range(N_Z)]
Z_GROUPS = [[p * N_Z + z for z in range(N_Z)] for p in range(N_XY)]
LANES = 128


def gelu_parts(pre_act):
    argument = root_coeff * (pre_act + cubic_coeff * pre_act * pre_act * pre_act)
    tangent = jnp.tanh(argument)
    output_value = 0.5 * pre_act * (1.0 + tangent)
    derivative = 0.5 * (1.0 + tangent) + 0.5 * pre_act * (1.0 - tangent * tangent) * root_coeff * (
        1.0 + 3.0 * cubic_coeff * pre_act * pre_act
    )
    return (output_value, derivative)


def swap_xy(block):
    return lax.all_to_all(block, "row", 0, 0, axis_index_groups=XY_GROUPS)


def swap_z(block):
    return lax.all_to_all(block, "row", 0, 0, axis_index_groups=Z_GROUPS)


def per_device(tokens, weight, bias, grad_out):
    rows, features = tokens.shape
    panel, hidden = weight.shape
    all_rows = rows * N_XY * N_Z
    f32, bf16 = jnp.float32, jnp.bfloat16

    with jax.named_scope("tokens_xy"):
        t = tokens.reshape(rows, N_XY, N_Z * panel).transpose(1, 0, 2)
        t = swap_xy(t.reshape(N_XY, -1, LANES))
    with jax.named_scope("tokens_z"):
        t = t.reshape(N_XY * rows, N_Z, panel).transpose(1, 0, 2)
        t = swap_z(t.reshape(N_Z, -1, LANES))
        t = t.reshape(N_Z, N_XY, rows, panel).transpose(1, 0, 2, 3)
        token_panel = t.reshape(all_rows, panel)
    with jax.named_scope("pre_dot"):
        partial = jnp.dot(token_panel, weight, preferred_element_type=f32).astype(bf16)
        partial = partial.reshape(N_XY, -1, LANES)
    with jax.named_scope("pre_xy"):
        partial = swap_xy(partial)
        partial = jnp.sum(partial.astype(f32), axis=0).astype(bf16)
    with jax.named_scope("pre_z"):
        partial = swap_z(partial.reshape(N_Z, -1, LANES))
        pre_act = jnp.sum(partial.astype(f32), axis=0)
    with jax.named_scope("gelu"):
        pre_act = (pre_act.reshape(rows, -1, LANES) + bias.reshape(-1, LANES)).reshape(-1, LANES)
        output_value, derivative = gelu_parts(pre_act)
        activation = output_value.astype(bf16).reshape(rows, hidden)
        grad_pre = (grad_out.reshape(-1, LANES).astype(f32) * derivative).astype(bf16)
    with jax.named_scope("grad_z"):
        g = swap_z(jnp.broadcast_to(grad_pre[None], (N_Z,) + grad_pre.shape))
    with jax.named_scope("grad_xy"):
        g = g.reshape(-1, LANES)
        g = swap_xy(jnp.broadcast_to(g[None], (N_XY,) + g.shape))
        g = g.reshape(all_rows, hidden)
    with jax.named_scope("input_dot"):
        part = lax.dot_general(g, weight, (((1,), (1,)), ((), ())), preferred_element_type=f32).astype(bf16)
    with jax.named_scope("input_col"):
        slim = panel // N_COL
        part = part.reshape(all_rows, N_COL, slim).transpose(1, 0, 2).reshape(N_COL, -1, LANES)
        part = lax.all_to_all(part, "col", 0, 0)
        part = jnp.sum(part.astype(f32), axis=0).astype(bf16)
    with jax.named_scope("input_row"):
        part = lax.all_to_all(part.reshape(N_XY * N_Z, rows * slim), "row", 0, 0)
    with jax.named_scope("input_back"):
        part = part.reshape(-1, LANES)
        part = lax.all_to_all(jnp.broadcast_to(part[None], (N_COL,) + part.shape), "col", 0, 0)
        part = part.reshape(N_COL, N_XY * N_Z, rows, slim).transpose(2, 1, 0, 3)
        input_grad = part.reshape(rows, features)
    with jax.named_scope("weight_dot"):
        weight_grad = lax.dot_general(token_panel, g, (((0,), (0,)), ((), ())), preferred_element_type=f32).astype(bf16)
    with jax.named_scope("bias_sum"):
        bias_grad = jnp.sum(g.astype(f32), axis=0)
    return (activation, input_grad, weight_grad, bias_grad)


def solution(mesh):
    placed = (P("row", None), P("row", "col"), P("col"), P("row", "col"))
    return jax.shard_map(
        per_device,
        mesh=mesh,
        in_specs=placed,
        out_specs=(P("row", "col"), P("row", None), P("row", "col"), P("col")),
        check_vma=False,
    )
```

```python
import math

import jax
import jax.numpy as jnp
from jax import lax
from jax.experimental import pallas as pl
from jax.experimental.pallas import tpu as pltpu
from jax.sharding import PartitionSpec as P

root_coeff = math.sqrt(2.0 / math.pi)
cubic_coeff = 0.044715

N_XY, N_Z, N_COL, N_ROW = 16, 4, 8, 64
LANES = 128
XY_GROUPS = [[p * N_Z + z for p in range(N_XY)] for z in range(N_Z)]
Z_GROUPS = [[p * N_Z + z for z in range(N_Z)] for p in range(N_XY)]
BOTH = ("row", "col")


def turned(row, chunk):
    low, core = divmod(chunk, 2)
    return row * N_COL + ((low + row) % 4) * 2 + core


ROW_GROUPS = [[turned(r, j) for r in range(N_ROW)] for j in range(N_COL)]
COL_GROUPS = [[turned(r, j) for j in range(N_COL)] for r in range(N_ROW)]


def gelu_parts(pre_act):
    argument = root_coeff * (pre_act + cubic_coeff * pre_act * pre_act * pre_act)
    tangent = jnp.tanh(argument)
    output_value = 0.5 * pre_act * (1.0 + tangent)
    derivative = 0.5 * (1.0 + tangent) + 0.5 * pre_act * (1.0 - tangent * tangent) * root_coeff * (
        1.0 + 3.0 * cubic_coeff * pre_act * pre_act
    )
    return (output_value, derivative)


def swap(block, axis, groups):
    return lax.all_to_all(block, axis, 0, 0, axis_index_groups=groups)


def in_vmem(value):
    return pltpu.with_memory_space_constraint(value, pltpu.VMEM)


WHOLE = pl.BlockSpec(memory_space=pltpu.VMEM)
PARAMS = pltpu.CompilerParams(vmem_limit_bytes=24 * 2**20)


def pre_kernel(t_ref, w_ref, o_ref, s_ref):
    rows, hidden = t_ref.shape[0], w_ref.shape[1]
    lines = hidden // LANES
    for j in range(0, lines, 2):
        both = jnp.dot(t_ref[...], w_ref[:, j * LANES : (j + 2) * LANES], preferred_element_type=jnp.float32)
        s_ref[pl.ds(j, rows, stride=lines), :] = both[:, :LANES]
        s_ref[pl.ds(j + 1, rows, stride=lines), :] = both[:, LANES:]
    o_ref[...] = s_ref[...].astype(o_ref.dtype).reshape(o_ref.shape)


def pre_dot(token_panel, weight):
    rows, hidden = token_panel.shape[0], weight.shape[1]
    lines = rows * hidden // LANES
    return pl.pallas_call(
        pre_kernel,
        out_shape=pltpu.VMEM((N_XY, lines // N_XY, LANES), jnp.bfloat16),
        in_specs=[WHOLE, WHOLE],
        out_specs=WHOLE,
        scratch_shapes=[pltpu.VMEM((lines, LANES), jnp.float32)],
        compiler_params=PARAMS,
        cost_estimate=pl.CostEstimate(flops=2 * rows * hidden * weight.shape[0], bytes_accessed=4 * 2**20, transcendentals=0),
        name="pre_dot",
    )(in_vmem(token_panel), weight)


def sum_kernel(x_ref, o_ref):
    step = 96
    for b in range(0, o_ref.shape[0], step):
        total = x_ref[0, b : b + step, :].astype(jnp.float32)
        for p in range(1, x_ref.shape[0]):
            total += x_ref[p, b : b + step, :].astype(jnp.float32)
        o_ref[b : b + step, :] = total.astype(o_ref.dtype)


def sum_parts(parts):
    return pl.pallas_call(
        sum_kernel,
        out_shape=pltpu.VMEM(parts.shape[1:], jnp.bfloat16),
        in_specs=[WHOLE],
        out_specs=WHOLE,
        compiler_params=PARAMS,
        cost_estimate=pl.CostEstimate(flops=parts.size, bytes_accessed=2 * parts.size, transcendentals=0),
        name="sum_parts",
    )(in_vmem(parts))


def post_kernel(g_ref, w_ref, rows_ref, part_ref, s_ref):
    rows, hidden = rows_ref.shape
    lines = hidden // LANES
    s_ref[...] = g_ref[...].reshape(s_ref.shape).astype(jnp.float32)
    for j in range(lines):
        rows_ref[:, j * LANES : (j + 1) * LANES] = s_ref[pl.ds(j, rows, stride=lines), :].astype(rows_ref.dtype)
    part_ref[...] = lax.dot_general(
        w_ref[...], rows_ref[...], (((1,), (1,)), ((), ())), preferred_element_type=jnp.float32
    ).astype(part_ref.dtype)


def post_dot(gathered, weight):
    panel, hidden = weight.shape
    rows = gathered.size // hidden
    return pl.pallas_call(
        post_kernel,
        out_shape=(pltpu.VMEM((rows, hidden), jnp.bfloat16), pltpu.VMEM((panel, rows), jnp.bfloat16)),
        in_specs=[WHOLE, WHOLE],
        out_specs=(WHOLE, WHOLE),
        scratch_shapes=[pltpu.VMEM((gathered.size // LANES, LANES), jnp.float32)],
        compiler_params=PARAMS,
        cost_estimate=pl.CostEstimate(flops=2 * rows * hidden * panel, bytes_accessed=6 * 2**20, transcendentals=0),
        name="post_dot",
    )(in_vmem(gathered), weight)


def per_device(tokens, weight, bias, grad_out):
    rows, features = tokens.shape
    panel, hidden = weight.shape
    all_rows = rows * N_ROW
    f32, bf16 = jnp.float32, jnp.bfloat16

    with jax.named_scope("tokens"):
        t = tokens.reshape(rows, N_ROW, panel).transpose(1, 0, 2)
        t = swap(t.reshape(N_ROW, 8, -1), BOTH, ROW_GROUPS)
        token_panel = t.reshape(all_rows, panel)
    with jax.named_scope("pre_dot"):
        partial = pre_dot(token_panel, weight)
    with jax.named_scope("pre_xy"):
        partial = swap(partial, "row", XY_GROUPS)
        partial = sum_parts(partial)
    with jax.named_scope("pre_z"):
        partial = swap(partial.reshape(N_Z, -1, LANES), "row", Z_GROUPS)
        pre_act = jnp.sum(partial.astype(f32), axis=0)
    with jax.named_scope("gelu"):
        pre_act = (pre_act.reshape(rows, -1, LANES) + bias.reshape(-1, LANES)).reshape(-1, LANES)
        output_value, derivative = gelu_parts(pre_act)
        activation = output_value.astype(bf16).reshape(rows, hidden)
        grad_pre = (grad_out.reshape(-1, LANES).astype(f32) * derivative).astype(bf16)
    with jax.named_scope("grad_z"):
        g = swap(jnp.broadcast_to(grad_pre[None], (N_Z,) + grad_pre.shape), "row", Z_GROUPS)
    with jax.named_scope("grad_xy"):
        g = g.reshape(-1, LANES)
        g = swap(jnp.broadcast_to(g[None], (N_XY,) + g.shape), "row", XY_GROUPS)
    with jax.named_scope("input_dot"):
        g, part = post_dot(g, weight)
    with jax.named_scope("input_col"):
        part = swap(part.reshape(N_COL, -1, all_rows), BOTH, COL_GROUPS)
        part = jnp.sum(part.astype(f32), axis=0).astype(bf16)
    with jax.named_scope("input_row"):
        slim = panel // N_COL
        part = part.reshape(slim, N_ROW, rows).transpose(1, 2, 0).reshape(N_ROW, rows * slim)
        part = swap(part, BOTH, ROW_GROUPS)
    with jax.named_scope("input_back"):
        part = part.reshape(N_ROW, rows, slim).transpose(1, 0, 2).reshape(-1, LANES)
        part = swap(jnp.broadcast_to(part[None], (N_COL,) + part.shape), BOTH, COL_GROUPS)
        part = part.reshape(N_COL, rows, N_ROW, slim).transpose(1, 2, 0, 3)
        input_grad = part.reshape(rows, features)
    with jax.named_scope("weight_dot"):
        weight_grad = lax.dot_general(token_panel, g, (((0,), (0,)), ((), ())), preferred_element_type=f32).astype(bf16)
    with jax.named_scope("bias_sum"):
        bias_grad = jnp.sum(g.astype(f32), axis=0)
    return (activation, input_grad, weight_grad, bias_grad)


def solution(mesh):
    placed = (P("row", None), P("row", "col"), P("col"), P("row", "col"))
    return jax.shard_map(
        per_device,
        mesh=mesh,
        in_specs=placed,
        out_specs=(P("row", "col"), P("row", None), P("row", "col"), P("col")),
        check_vma=False,
    )
```

```python
import functools
import math

import jax
import jax.numpy as jnp
from jax import lax
from jax.experimental import pallas as pl
from jax.experimental.pallas import tpu as pltpu
from jax.sharding import PartitionSpec as P

root_coeff = math.sqrt(2.0 / math.pi)
cubic_coeff = 0.044715

N_PAIR, N_HALF, N_YZ, N_Z, N_COL, N_ROW = 2, 2, 16, 4, 8, 64
N_PY = 8
LANES = 128
TAIL = 16
BOTH = ("row", "col")


def row_of(pair, half, yz):
    return (pair * N_HALF + half) * N_YZ + yz


def turned(row, chunk):
    low, core = divmod(chunk, 2)
    return row * N_COL + ((low + row) % 4) * 2 + core


ROW_GROUPS = [[turned(r, j) for r in range(N_ROW)] for j in range(N_COL)]
COL_GROUPS = [[turned(r, j) for j in range(N_COL)] for r in range(N_ROW)]
PAIR_COL_GROUPS = [
    [turned(row_of(p, i, yz), j) for i in range(N_HALF) for j in range(N_COL)] for p in range(N_PAIR) for yz in range(N_YZ)
]
PY_GROUPS = [
    [row_of(p, i, y * N_Z + z) for p in range(N_PAIR) for y in range(N_YZ // N_Z)] for i in range(N_HALF) for z in range(N_Z)
]
Z_GROUPS = [[q * N_Z + z for z in range(N_Z)] for q in range(N_ROW // N_Z)]
PARTNER = [(r, r ^ N_YZ) for r in range(N_ROW)]


def gelu_parts(pre_act):
    argument = root_coeff * (pre_act + cubic_coeff * pre_act * pre_act * pre_act)
    tangent = jnp.tanh(argument)
    output_value = 0.5 * pre_act * (1.0 + tangent)
    derivative = 0.5 * (1.0 + tangent) + 0.5 * pre_act * (1.0 - tangent * tangent) * root_coeff * (
        1.0 + 3.0 * cubic_coeff * pre_act * pre_act
    )
    return (output_value, derivative)


def swap(block, axis, groups):
    return lax.all_to_all(block, axis, 0, 0, axis_index_groups=groups)


def in_vmem(value):
    return pltpu.with_memory_space_constraint(value, pltpu.VMEM)


WHOLE = pl.BlockSpec(memory_space=pltpu.VMEM)
SCALAR = pl.BlockSpec(memory_space=pltpu.SMEM)
PARAMS = pltpu.CompilerParams(vmem_limit_bytes=24 * 2**20)


def weight_kernel(half_ref, w_ref, got_ref, o_ref):
    panel, width = o_ref.shape[1:]
    o_ref[0] = w_ref[:, pl.ds(pl.multiple_of(half_ref[0] * width, LANES), width)]
    o_ref[1] = got_ref[:panel, :]


def both_panels(half, weight, got):
    panel, width = weight.shape[0], got.shape[1]
    return pl.pallas_call(
        weight_kernel,
        out_shape=pltpu.VMEM((N_HALF, panel, width), jnp.bfloat16),
        in_specs=[SCALAR, WHOLE, WHOLE],
        out_specs=WHOLE,
        compiler_params=PARAMS,
        cost_estimate=pl.CostEstimate(flops=0, bytes_accessed=3 * 2**20, transcendentals=0),
        name="both_panels",
    )(half, weight, got)


def pre_kernel(own_ref, other_ref, w_ref, o_ref, s_ref):
    rows = own_ref.shape[0]
    lines = w_ref.shape[2] // LANES
    for j in range(0, lines, 2):
        columns = slice(j * LANES, (j + 2) * LANES)
        both = jnp.dot(own_ref[...], w_ref[0, :, columns], preferred_element_type=jnp.float32)
        both += jnp.dot(other_ref[...], w_ref[1, :, columns], preferred_element_type=jnp.float32)
        s_ref[pl.ds(j, rows, stride=lines), :] = both[:, :LANES]
        s_ref[pl.ds(j + 1, rows, stride=lines), :] = both[:, LANES:]
    o_ref[...] = s_ref[...].astype(o_ref.dtype).reshape(o_ref.shape)


def pre_dot(own, other, weights):
    rows, (_, panel, width) = own.shape[0], weights.shape
    lines = rows * width // LANES
    return pl.pallas_call(
        pre_kernel,
        out_shape=pltpu.VMEM((N_PY, lines // N_PY, LANES), jnp.bfloat16),
        in_specs=[WHOLE, WHOLE, WHOLE],
        out_specs=WHOLE,
        scratch_shapes=[pltpu.VMEM((lines, LANES), jnp.float32)],
        compiler_params=PARAMS,
        cost_estimate=pl.CostEstimate(flops=4 * rows * width * panel, bytes_accessed=4 * 2**20, transcendentals=0),
        name="pre_dot",
    )(in_vmem(own), in_vmem(other), in_vmem(weights))


def sum_kernel(x_ref, o_ref):
    step = 96
    for b in range(0, o_ref.shape[0], step):
        total = x_ref[0, b : b + step, :].astype(jnp.float32)
        for p in range(1, x_ref.shape[0]):
            total += x_ref[p, b : b + step, :].astype(jnp.float32)
        o_ref[b : b + step, :] = total.astype(o_ref.dtype)


def sum_parts(parts):
    return pl.pallas_call(
        sum_kernel,
        out_shape=pltpu.VMEM(parts.shape[1:], jnp.bfloat16),
        in_specs=[WHOLE],
        out_specs=WHOLE,
        compiler_params=PARAMS,
        cost_estimate=pl.CostEstimate(flops=parts.size, bytes_accessed=2 * parts.size, transcendentals=0),
        name="sum_parts",
    )(in_vmem(parts))


def post_kernel(half_ref, g_ref, w_ref, rows_ref, part_ref, s_ref):
    rows, width = rows_ref.shape
    lines = width // LANES
    s_ref[...] = g_ref[...].reshape(s_ref.shape).astype(jnp.float32)
    for j in range(lines):
        rows_ref[:, j * LANES : (j + 1) * LANES] = s_ref[pl.ds(j, rows, stride=lines), :].astype(rows_ref.dtype)
    for k, place in enumerate((half_ref[0], 1 - half_ref[0])):
        part_ref[place] = lax.dot_general(
            w_ref[k], rows_ref[...], (((1,), (1,)), ((), ())), preferred_element_type=jnp.float32
        ).astype(part_ref.dtype)


def post_dot(half, gathered, weights):
    _, panel, width = weights.shape
    rows = gathered.size // width
    return pl.pallas_call(
        post_kernel,
        out_shape=(pltpu.VMEM((rows, width), jnp.bfloat16), jax.ShapeDtypeStruct((N_HALF, panel, rows), jnp.bfloat16)),
        in_specs=[SCALAR, WHOLE, WHOLE],
        out_specs=(WHOLE, WHOLE),
        scratch_shapes=[pltpu.VMEM((gathered.size // LANES, LANES), jnp.float32)],
        compiler_params=PARAMS,
        cost_estimate=pl.CostEstimate(flops=4 * rows * width * panel, bytes_accessed=6 * 2**20, transcendentals=0),
        name="post_dot",
    )(half, in_vmem(gathered), in_vmem(weights))


def join_kernel(half_ref, w_ref, act_ref, bias_ref, back_ref, w_out, act_out, bias_out):
    panel, width = w_ref.shape
    rows = act_ref.shape[0]
    mine = pl.ds(pl.multiple_of(half_ref[0] * width, LANES), width)
    theirs = pl.ds(pl.multiple_of((1 - half_ref[0]) * width, LANES), width)
    w_out[:, mine] = w_ref[...]
    w_out[:, theirs] = back_ref[:panel, :]
    tail = back_ref[panel:, :].astype(jnp.float32)
    act_out[:, mine] = act_ref[...]
    act_out[:, theirs] = tail[:rows].astype(act_out.dtype)
    bias_out[:, mine] = bias_ref[...]
    bias_out[:, theirs] = tail[rows : rows + 1] + tail[rows + 1 : rows + 2] + tail[rows + 2 : rows + 3]


def join_halves(half, weight_own, act_own, bias_own, back):
    panel, width = weight_own.shape
    hidden, rows = N_HALF * width, act_own.shape[0]
    return pl.pallas_call(
        join_kernel,
        out_shape=(
            jax.ShapeDtypeStruct((panel, hidden), jnp.bfloat16),
            jax.ShapeDtypeStruct((rows, hidden), jnp.bfloat16),
            jax.ShapeDtypeStruct((1, hidden), jnp.float32),
        ),
        in_specs=[SCALAR, WHOLE, WHOLE, WHOLE, WHOLE],
        out_specs=(WHOLE, WHOLE, WHOLE),
        compiler_params=PARAMS,
        cost_estimate=pl.CostEstimate(flops=2**20, bytes_accessed=3 * 2**20, transcendentals=0),
        name="join_halves",
    )(half, weight_own, act_own, bias_own, back)


def interleave_kernel(slim, x_ref, o_ref, s_ref):
    groups, lines = x_ref.shape[0], x_ref.shape[1]
    rows = o_ref.shape[0]
    step = lines // rows
    s_ref[...] = x_ref[...].astype(jnp.float32)
    values = [
        jnp.concatenate([s_ref[c, pl.ds(m, rows, stride=step), :] for m in range(step)], 1) for c in range(groups)
    ]
    for r in range(0, N_ROW, 2):
        pieces = [values[c][:, q * slim : (q + 1) * slim] for q in (r, r + 1) for c in range(groups)]
        width = len(pieces) * slim
        o_ref[:, r // 2 * width : (r // 2 + 1) * width] = jnp.concatenate(pieces, 1).astype(o_ref.dtype)


def interleave(parts, rows, slim):
    groups, lines, _ = parts.shape
    return pl.pallas_call(
        functools.partial(interleave_kernel, slim),
        out_shape=jax.ShapeDtypeStruct((rows, groups * lines // rows * LANES), jnp.bfloat16),
        in_specs=[WHOLE],
        out_specs=WHOLE,
        scratch_shapes=[pltpu.VMEM((groups, lines, LANES), jnp.float32)],
        compiler_params=PARAMS,
        cost_estimate=pl.CostEstimate(flops=2**20, bytes_accessed=2**19, transcendentals=0),
        name="interleave",
    )(parts)


def per_device(tokens, weight, bias, grad_out):
    rows, features = tokens.shape
    panel, hidden = weight.shape
    all_rows = rows * N_ROW
    width = hidden // N_HALF
    f32, bf16 = jnp.float32, jnp.bfloat16
    half = (lax.axis_index("row") // N_YZ) % N_HALF
    first = half == 0
    half_ref = half.reshape(1).astype(jnp.int32)

    def columns(value, which):
        return lax.dynamic_slice_in_dim(value, which * width, width, value.ndim - 1)

    def in_order(own, other, axis):
        return jnp.concatenate([jnp.where(first, own, other), jnp.where(first, other, own)], axis)

    with jax.named_scope("weight_in"):
        give = jnp.concatenate([columns(weight, 1 - half), columns(grad_out, 1 - half)], 0)
        got = lax.ppermute(give, "row", PARTNER)
        weights = both_panels(half_ref, weight, got)
    with jax.named_scope("tokens"):
        t = tokens.reshape(rows, N_ROW, panel).transpose(1, 0, 2).reshape(N_ROW, 8, -1)
        flipped = t.reshape(N_PAIR, N_HALF, N_YZ, 8, -1)[:, ::-1].reshape(t.shape)
        t = swap(jnp.concatenate([t, flipped], 1), BOTH, ROW_GROUPS)

        def token_rows(value):
            value = value.reshape(N_PAIR, N_HALF, N_YZ, rows, panel).transpose(0, 2, 1, 3, 4)
            return value.reshape(all_rows, panel)

        own, other = token_rows(t[:, :8]), token_rows(t[:, 8:])
    with jax.named_scope("pre_dot"):
        partial = pre_dot(own, other, weights)
    with jax.named_scope("pre_xy"):
        partial = swap(partial, "row", PY_GROUPS)
        partial = sum_parts(partial)
    with jax.named_scope("pre_z"):
        partial = swap(partial.reshape(N_Z, -1, LANES), "row", Z_GROUPS)
        pre_act = jnp.sum(partial.astype(f32), axis=0)
    with jax.named_scope("gelu"):
        pair_rows = N_HALF * rows
        bias_half = columns(bias, half).reshape(-1, LANES)
        pre_act = (pre_act.reshape(pair_rows, -1, LANES) + bias_half).reshape(-1, LANES)
        output_value, derivative = gelu_parts(pre_act)
        activation = output_value.astype(bf16)
        upstream = in_order(columns(grad_out, half), got[panel:], 0).reshape(-1, LANES)
        grad_pre = (upstream.astype(f32) * derivative).astype(bf16)
        activation, grad_pre = lax.optimization_barrier((activation, grad_pre))
    with jax.named_scope("grad_z"):
        g = swap(jnp.broadcast_to(grad_pre[None], (N_Z,) + grad_pre.shape), "row", Z_GROUPS)
    with jax.named_scope("grad_xy"):
        g = g.reshape(-1, LANES)
        g = swap(jnp.broadcast_to(g[None], (N_PY,) + g.shape), "row", PY_GROUPS)
        g, activation = lax.optimization_barrier((g, activation))
        activation = activation.reshape(N_HALF, rows, width)
    with jax.named_scope("input_dot"):
        g, part = post_dot(half_ref, g, weights)
    with jax.named_scope("weight_dot"):
        over_rows = (((0,), (0,)), ((), ()))
        weight_own = lax.dot_general(own, g, over_rows, preferred_element_type=f32).astype(bf16)
        weight_other = lax.dot_general(other, g, over_rows, preferred_element_type=f32).astype(bf16)
    with jax.named_scope("bias_sum"):
        bias_half = jnp.sum(g.astype(f32), axis=0)
        high = lax.reduce_precision(bias_half, 8, 7)
        middle = lax.reduce_precision(bias_half - high, 8, 7)
        low = bias_half - high - middle
        pieces = jnp.stack([high, middle, low] + [jnp.zeros_like(low)] * (TAIL - rows - 3)).astype(bf16)
    with jax.named_scope("input_col"):
        slim = panel // N_COL
        part = swap(part.reshape(N_HALF * N_COL, slim, all_rows), BOTH, PAIR_COL_GROUPS)
        part = jnp.sum(part.astype(f32), axis=0).astype(bf16)
    with jax.named_scope("weight_out"):
        give = jnp.concatenate([weight_other, lax.dynamic_index_in_dim(activation, 1 - half, 0, False), pieces], 0)
        part, give = lax.optimization_barrier((part, give))
        back = lax.ppermute(give, "row", PARTNER)
    with jax.named_scope("input_row"):
        part = part.reshape(slim, N_PAIR, N_YZ, N_HALF, rows).transpose(1, 3, 2, 4, 0).reshape(N_ROW, rows * slim)
        part = swap(part, BOTH, ROW_GROUPS)
    with jax.named_scope("input_back"):
        part = part.reshape(N_ROW, rows, slim).transpose(1, 0, 2).reshape(-1, LANES)
        part = swap(jnp.broadcast_to(part[None], (N_COL,) + part.shape), BOTH, COL_GROUPS)
        act_own = lax.dynamic_index_in_dim(activation, half, 0, False)
        outs = join_halves(half_ref, weight_own, act_own, bias_half.reshape(1, -1), back)
        part, weight_grad, activation, bias_grad = lax.optimization_barrier((part,) + tuple(outs))
        bias_grad = bias_grad.reshape(hidden)
        input_grad = interleave(part, rows, slim)
    return (activation, input_grad, weight_grad, bias_grad)


def solution(mesh):
    placed = (P("row", None), P("row", "col"), P("col"), P("row", "col"))
    return jax.shard_map(
        per_device,
        mesh=mesh,
        in_specs=placed,
        out_specs=(P("row", "col"), P("row", None), P("row", "col"), P("col")),
        check_vma=False,
    )
```

```python
import functools
import math

import jax
import jax.numpy as jnp
from jax import lax
from jax.experimental import pallas as pl
from jax.experimental.pallas import tpu as pltpu
from jax.sharding import PartitionSpec as P

root_coeff = math.sqrt(2.0 / math.pi)
cubic_coeff = 0.044715

N_PAIR, N_HALF, N_YZ, N_Z, N_COL, N_ROW = 2, 2, 16, 4, 8, 64
N_PY = 8
LANES = 128
TAIL = 16
BOTH = ("row", "col")


def row_of(pair, half, yz):
    return (pair * N_HALF + half) * N_YZ + yz


def turned(row, chunk):
    low, core = divmod(chunk, 2)
    return row * N_COL + ((low + row) % 4) * 2 + core


ROW_GROUPS = [[turned(r, j) for r in range(N_ROW)] for j in range(N_COL)]
COL_GROUPS = [[turned(r, j) for j in range(N_COL)] for r in range(N_ROW)]
PAIR_COL_GROUPS = [
    [turned(row_of(p, i, yz), j) for i in range(N_HALF) for j in range(N_COL)] for p in range(N_PAIR) for yz in range(N_YZ)
]
PY_GROUPS = [
    [row_of(p, i, y * N_Z + z) for p in range(N_PAIR) for y in range(N_YZ // N_Z)] for i in range(N_HALF) for z in range(N_Z)
]
Z_GROUPS = [[q * N_Z + z for z in range(N_Z)] for q in range(N_ROW // N_Z)]
PARTNER = [(r, r ^ N_YZ) for r in range(N_ROW)]


def gelu_parts(pre_act):
    argument = root_coeff * (pre_act + cubic_coeff * pre_act * pre_act * pre_act)
    tangent = jnp.tanh(argument)
    output_value = 0.5 * pre_act * (1.0 + tangent)
    derivative = 0.5 * (1.0 + tangent) + 0.5 * pre_act * (1.0 - tangent * tangent) * root_coeff * (
        1.0 + 3.0 * cubic_coeff * pre_act * pre_act
    )
    return (output_value, derivative)


def swap(block, axis, groups):
    return lax.all_to_all(block, axis, 0, 0, axis_index_groups=groups)


def in_vmem(value):
    return pltpu.with_memory_space_constraint(value, pltpu.VMEM)


WHOLE = pl.BlockSpec(memory_space=pltpu.VMEM)
SCALAR = pl.BlockSpec(memory_space=pltpu.SMEM)
PARAMS = pltpu.CompilerParams(vmem_limit_bytes=24 * 2**20)


def weight_kernel(half_ref, w_ref, got_ref, o_ref):
    panel, width = o_ref.shape[1:]
    o_ref[0] = w_ref[:, pl.ds(pl.multiple_of(half_ref[0] * width, LANES), width)]
    o_ref[1] = got_ref[:panel, :]


def both_panels(half, weight, got):
    panel, width = weight.shape[0], got.shape[1]
    return pl.pallas_call(
        weight_kernel,
        out_shape=pltpu.VMEM((N_HALF, panel, width), jnp.bfloat16),
        in_specs=[SCALAR, WHOLE, WHOLE],
        out_specs=WHOLE,
        compiler_params=PARAMS,
        cost_estimate=pl.CostEstimate(flops=0, bytes_accessed=3 * 2**20, transcendentals=0),
        name="both_panels",
    )(half, weight, got)


def pre_kernel(own_ref, other_ref, w_ref, o_ref, s_ref):
    rows = own_ref.shape[0]
    lines = w_ref.shape[2] // LANES
    for j in range(0, lines, 2):
        columns = slice(j * LANES, (j + 2) * LANES)
        both = jnp.dot(own_ref[...], w_ref[0, :, columns], preferred_element_type=jnp.float32)
        both += jnp.dot(other_ref[...], w_ref[1, :, columns], preferred_element_type=jnp.float32)
        s_ref[pl.ds(j, rows, stride=lines), :] = both[:, :LANES]
        s_ref[pl.ds(j + 1, rows, stride=lines), :] = both[:, LANES:]
    o_ref[...] = s_ref[...].astype(o_ref.dtype).reshape(o_ref.shape)


def pre_dot(own, other, weights):
    rows, (_, panel, width) = own.shape[0], weights.shape
    lines = rows * width // LANES
    return pl.pallas_call(
        pre_kernel,
        out_shape=pltpu.VMEM((N_PY, lines // N_PY, LANES), jnp.bfloat16),
        in_specs=[WHOLE, WHOLE, WHOLE],
        out_specs=WHOLE,
        scratch_shapes=[pltpu.VMEM((lines, LANES), jnp.float32)],
        compiler_params=PARAMS,
        cost_estimate=pl.CostEstimate(flops=4 * rows * width * panel, bytes_accessed=4 * 2**20, transcendentals=0),
        name="pre_dot",
    )(in_vmem(own), in_vmem(other), in_vmem(weights))


def sum_kernel(x_ref, o_ref):
    step = 96
    for b in range(0, o_ref.shape[0], step):
        total = x_ref[0, b : b + step, :].astype(jnp.float32)
        for p in range(1, x_ref.shape[0]):
            total += x_ref[p, b : b + step, :].astype(jnp.float32)
        o_ref[b : b + step, :] = total.astype(o_ref.dtype)


def sum_parts(parts):
    return pl.pallas_call(
        sum_kernel,
        out_shape=pltpu.VMEM(parts.shape[1:], jnp.bfloat16),
        in_specs=[WHOLE],
        out_specs=WHOLE,
        compiler_params=PARAMS,
        cost_estimate=pl.CostEstimate(flops=parts.size, bytes_accessed=2 * parts.size, transcendentals=0),
        name="sum_parts",
    )(in_vmem(parts))


def post_kernel(half_ref, g_ref, w_ref, rows_ref, part_ref, s_ref):
    rows, width = rows_ref.shape
    lines = width // LANES
    s_ref[...] = g_ref[...].reshape(s_ref.shape).astype(jnp.float32)
    for j in range(lines):
        rows_ref[:, j * LANES : (j + 1) * LANES] = s_ref[pl.ds(j, rows, stride=lines), :].astype(rows_ref.dtype)
    for k, place in enumerate((half_ref[0], 1 - half_ref[0])):
        part_ref[place] = lax.dot_general(
            w_ref[k], rows_ref[...], (((1,), (1,)), ((), ())), preferred_element_type=jnp.float32
        ).astype(part_ref.dtype)


def post_dot(half, gathered, weights):
    _, panel, width = weights.shape
    rows = gathered.size // width
    return pl.pallas_call(
        post_kernel,
        out_shape=(pltpu.VMEM((rows, width), jnp.bfloat16), jax.ShapeDtypeStruct((N_HALF, panel, rows), jnp.bfloat16)),
        in_specs=[SCALAR, WHOLE, WHOLE],
        out_specs=(WHOLE, WHOLE),
        scratch_shapes=[pltpu.VMEM((gathered.size // LANES, LANES), jnp.float32)],
        compiler_params=PARAMS,
        cost_estimate=pl.CostEstimate(flops=4 * rows * width * panel, bytes_accessed=6 * 2**20, transcendentals=0),
        name="post_dot",
    )(half, in_vmem(gathered), in_vmem(weights))


def join_kernel(half_ref, w_ref, act_ref, bias_ref, back_ref, w_out, act_out, bias_out):
    panel, width = w_ref.shape
    rows = act_ref.shape[0]
    mine = pl.ds(pl.multiple_of(half_ref[0] * width, LANES), width)
    theirs = pl.ds(pl.multiple_of((1 - half_ref[0]) * width, LANES), width)
    w_out[:, mine] = w_ref[...]
    w_out[:, theirs] = back_ref[:panel, :]
    tail = back_ref[panel:, :].astype(jnp.float32)
    act_out[:, mine] = act_ref[...]
    act_out[:, theirs] = tail[:rows].astype(act_out.dtype)
    bias_out[:, mine] = bias_ref[...]
    bias_out[:, theirs] = tail[rows : rows + 1] + tail[rows + 1 : rows + 2] + tail[rows + 2 : rows + 3]


def join_halves(half, weight_own, act_own, bias_own, back):
    panel, width = weight_own.shape
    hidden, rows = N_HALF * width, act_own.shape[0]
    return pl.pallas_call(
        join_kernel,
        out_shape=(
            jax.ShapeDtypeStruct((panel, hidden), jnp.bfloat16),
            jax.ShapeDtypeStruct((rows, hidden), jnp.bfloat16),
            jax.ShapeDtypeStruct((1, hidden), jnp.float32),
        ),
        in_specs=[SCALAR, WHOLE, WHOLE, WHOLE, WHOLE],
        out_specs=(WHOLE, WHOLE, WHOLE),
        compiler_params=PARAMS,
        cost_estimate=pl.CostEstimate(flops=2**20, bytes_accessed=3 * 2**20, transcendentals=0),
        name="join_halves",
    )(half, weight_own, act_own, bias_own, back)


def interleave_kernel(slim, x_ref, o_ref, s_ref):
    groups, lines = x_ref.shape[0], x_ref.shape[1]
    rows = o_ref.shape[0]
    step = lines // rows
    s_ref[...] = x_ref[...].astype(jnp.float32)
    values = [
        jnp.concatenate([s_ref[c, pl.ds(m, rows, stride=step), :] for m in range(step)], 1) for c in range(groups)
    ]
    for r in range(0, N_ROW, 2):
        pieces = [values[c][:, q * slim : (q + 1) * slim] for q in (r, r + 1) for c in range(groups)]
        width = len(pieces) * slim
        o_ref[:, r // 2 * width : (r // 2 + 1) * width] = jnp.concatenate(pieces, 1).astype(o_ref.dtype)


def interleave(parts, rows, slim):
    groups, lines, _ = parts.shape
    return pl.pallas_call(
        functools.partial(interleave_kernel, slim),
        out_shape=jax.ShapeDtypeStruct((rows, groups * lines // rows * LANES), jnp.bfloat16),
        in_specs=[WHOLE],
        out_specs=WHOLE,
        scratch_shapes=[pltpu.VMEM((groups, lines, LANES), jnp.float32)],
        compiler_params=PARAMS,
        cost_estimate=pl.CostEstimate(flops=2**20, bytes_accessed=2**19, transcendentals=0),
        name="interleave",
    )(parts)


def per_device(tokens, weight, bias, grad_out):
    rows, features = tokens.shape
    panel, hidden = weight.shape
    all_rows = rows * N_ROW
    width = hidden // N_HALF
    f32, bf16 = jnp.float32, jnp.bfloat16
    half = (lax.axis_index("row") // N_YZ) % N_HALF
    first = half == 0
    half_ref = half.reshape(1).astype(jnp.int32)

    def columns(value, which):
        return lax.dynamic_slice_in_dim(value, which * width, width, value.ndim - 1)

    def in_order(own, other, axis):
        return jnp.concatenate([jnp.where(first, own, other), jnp.where(first, other, own)], axis)

    with jax.named_scope("weight_in"):
        give = jnp.concatenate([columns(weight, 1 - half), columns(grad_out, 1 - half)], 0)
        got = lax.ppermute(give, "row", PARTNER)
        weights = both_panels(half_ref, weight, got)
    with jax.named_scope("tokens"):
        t = tokens.reshape(rows, N_ROW, panel).transpose(1, 0, 2).reshape(N_ROW, 8, -1)
        flipped = t.reshape(N_PAIR, N_HALF, N_YZ, 8, -1)[:, ::-1].reshape(t.shape)
        t = swap(jnp.concatenate([t, flipped], 1), BOTH, ROW_GROUPS)

        def token_rows(value):
            value = value.reshape(N_PAIR, N_HALF, N_YZ, rows, panel).transpose(0, 2, 1, 3, 4)
            return value.reshape(all_rows, panel)

        own, other = token_rows(t[:, :8]), token_rows(t[:, 8:])
    with jax.named_scope("pre_dot"):
        pair_rows = N_HALF * rows
        bias_half = columns(bias, half).reshape(1, -1, LANES)
        bias_rows = jnp.broadcast_to(bias_half, (pair_rows,) + bias_half.shape[1:]).reshape(-1, LANES)
        upstream = in_order(columns(grad_out, half), got[panel:], 0).reshape(-1, LANES)
        own, other, bias_rows, upstream = lax.optimization_barrier((own, other, bias_rows, upstream))
        partial = pre_dot(own, other, weights)
    with jax.named_scope("pre_xy"):
        partial = swap(partial, "row", PY_GROUPS)
        partial = sum_parts(partial)
    with jax.named_scope("pre_z"):
        partial = swap(partial.reshape(N_Z, -1, LANES), "row", Z_GROUPS)
        pre_act = jnp.sum(partial.astype(f32), axis=0)
    with jax.named_scope("gelu"):
        pre_act = pre_act + bias_rows
        output_value, derivative = gelu_parts(pre_act)
        activation = output_value.astype(bf16)
        grad_pre = (upstream.astype(f32) * derivative).astype(bf16)
        activation, grad_pre = lax.optimization_barrier((activation, grad_pre))
    with jax.named_scope("grad_z"):
        g = swap(jnp.broadcast_to(grad_pre[None], (N_Z,) + grad_pre.shape), "row", Z_GROUPS)
    with jax.named_scope("grad_xy"):
        g = g.reshape(-1, LANES)
        g = swap(jnp.broadcast_to(g[None], (N_PY,) + g.shape), "row", PY_GROUPS)
        g, activation = lax.optimization_barrier((g, activation))
        activation = activation.reshape(N_HALF, rows, width)
    with jax.named_scope("input_dot"):
        g, part = post_dot(half_ref, g, weights)
    with jax.named_scope("weight_dot"):
        over_rows = (((0,), (0,)), ((), ()))
        weight_own = lax.dot_general(own, g, over_rows, preferred_element_type=f32).astype(bf16)
        weight_other = lax.dot_general(other, g, over_rows, preferred_element_type=f32).astype(bf16)
    with jax.named_scope("bias_sum"):
        bias_half = jnp.sum(g.astype(f32), axis=0)
        high = lax.reduce_precision(bias_half, 8, 7)
        middle = lax.reduce_precision(bias_half - high, 8, 7)
        low = bias_half - high - middle
        pieces = jnp.stack([high, middle, low] + [jnp.zeros_like(low)] * (TAIL - rows - 3)).astype(bf16)
    with jax.named_scope("input_col"):
        slim = panel // N_COL
        part = swap(part.reshape(N_HALF * N_COL, slim, all_rows), BOTH, PAIR_COL_GROUPS)
        part = jnp.sum(part.astype(f32), axis=0).astype(bf16)
    with jax.named_scope("weight_out"):
        give = jnp.concatenate([weight_other, lax.dynamic_index_in_dim(activation, 1 - half, 0, False), pieces], 0)
        part, give = lax.optimization_barrier((part, give))
        back = lax.ppermute(give, "row", PARTNER)
    with jax.named_scope("input_row"):
        part = part.reshape(slim, N_PAIR, N_YZ, N_HALF, rows).transpose(1, 3, 2, 4, 0).reshape(N_ROW, rows * slim)
        part = swap(part, BOTH, ROW_GROUPS)
    with jax.named_scope("input_back"):
        part = part.reshape(N_ROW, rows, slim).transpose(1, 0, 2).reshape(-1, LANES)
        part = swap(jnp.broadcast_to(part[None], (N_COL,) + part.shape), BOTH, COL_GROUPS)
        act_own = lax.dynamic_index_in_dim(activation, half, 0, False)
        outs = join_halves(half_ref, weight_own, act_own, bias_half.reshape(1, -1), back)
        part, weight_grad, activation, bias_grad = lax.optimization_barrier((part,) + tuple(outs))
        bias_grad = bias_grad.reshape(hidden)
        input_grad = interleave(part, rows, slim)
    return (activation, input_grad, weight_grad, bias_grad)


def solution(mesh):
    placed = (P("row", None), P("row", "col"), P("col"), P("row", "col"))
    return jax.shard_map(
        per_device,
        mesh=mesh,
        in_specs=placed,
        out_specs=(P("row", "col"), P("row", None), P("row", "col"), P("col")),
        check_vma=False,
    )
```

```python
import functools
import math

import jax
import jax.numpy as jnp
from jax import lax
from jax.experimental import pallas as pl
from jax.experimental.pallas import tpu as pltpu
from jax.sharding import PartitionSpec as P

root_coeff = math.sqrt(2.0 / math.pi)
cubic_coeff = 0.044715

N_PAIR, N_HALF, N_YZ, N_Z, N_COL, N_ROW = 2, 2, 16, 4, 8, 64
N_PY = 8
LANES = 128
TAIL = 16
BOTH = ("row", "col")


def row_of(pair, half, yz):
    return (pair * N_HALF + half) * N_YZ + yz


def turned(row, chunk):
    low, core = divmod(chunk, 2)
    return row * N_COL + ((low + row) % 4) * 2 + core


ROW_GROUPS = [[turned(r, j) for r in range(N_ROW)] for j in range(N_COL)]
COL_GROUPS = [[turned(r, j) for j in range(N_COL)] for r in range(N_ROW)]
PAIR_COL_GROUPS = [
    [turned(row_of(p, i, yz), j) for i in range(N_HALF) for j in range(N_COL)] for p in range(N_PAIR) for yz in range(N_YZ)
]
PY_GROUPS = [
    [row_of(p, i, y * N_Z + z) for p in range(N_PAIR) for y in range(N_YZ // N_Z)] for i in range(N_HALF) for z in range(N_Z)
]
Z_GROUPS = [[q * N_Z + z for z in range(N_Z)] for q in range(N_ROW // N_Z)]
CORES = [(c, c ^ 1) for c in range(N_COL)]
PARTNER = [(r, r ^ N_YZ) for r in range(N_ROW)]


def gelu_parts(pre_act):
    argument = root_coeff * (pre_act + cubic_coeff * pre_act * pre_act * pre_act)
    tangent = jnp.tanh(argument)
    output_value = 0.5 * pre_act * (1.0 + tangent)
    derivative = 0.5 * (1.0 + tangent) + 0.5 * pre_act * (1.0 - tangent * tangent) * root_coeff * (
        1.0 + 3.0 * cubic_coeff * pre_act * pre_act
    )
    return (output_value, derivative)


def swap(block, axis, groups):
    return lax.all_to_all(block, axis, 0, 0, axis_index_groups=groups)


def in_vmem(value):
    return pltpu.with_memory_space_constraint(value, pltpu.VMEM)


WHOLE = pl.BlockSpec(memory_space=pltpu.VMEM)
SCALAR = pl.BlockSpec(memory_space=pltpu.SMEM)
PARAMS = pltpu.CompilerParams(vmem_limit_bytes=24 * 2**20)


def weight_kernel(half_ref, w_ref, got_ref, o_ref):
    panel, width = o_ref.shape[1:]
    o_ref[half_ref[1]] = w_ref[:, pl.ds(pl.multiple_of(half_ref[0] * width, LANES), width)]
    o_ref[1 - half_ref[1]] = got_ref[:panel, :]


def both_panels(half, weight, got):
    panel, width = weight.shape[0], got.shape[1]
    return pl.pallas_call(
        weight_kernel,
        out_shape=pltpu.VMEM((N_HALF, panel, width), jnp.bfloat16),
        in_specs=[SCALAR, WHOLE, WHOLE],
        out_specs=WHOLE,
        compiler_params=PARAMS,
        cost_estimate=pl.CostEstimate(flops=0, bytes_accessed=3 * 2**20, transcendentals=0),
        name="both_panels",
    )(half, weight, got)


def pre_kernel(own_ref, other_ref, w_ref, o_ref, s_ref):
    rows = own_ref.shape[0]
    lines = w_ref.shape[2] // LANES
    for j in range(0, lines, 2):
        columns = slice(j * LANES, (j + 2) * LANES)
        both = jnp.dot(own_ref[...], w_ref[0, :, columns], preferred_element_type=jnp.float32)
        both += jnp.dot(other_ref[...], w_ref[1, :, columns], preferred_element_type=jnp.float32)
        s_ref[pl.ds(j, rows, stride=lines), :] = both[:, :LANES]
        s_ref[pl.ds(j + 1, rows, stride=lines), :] = both[:, LANES:]
    o_ref[...] = s_ref[...].astype(o_ref.dtype).reshape(o_ref.shape)


def pre_dot(own, other, weights):
    rows, (_, panel, width) = own.shape[0], weights.shape
    lines = rows * width // LANES
    return pl.pallas_call(
        pre_kernel,
        out_shape=pltpu.VMEM((N_PY, lines // N_PY, LANES), jnp.bfloat16),
        in_specs=[WHOLE, WHOLE, WHOLE],
        out_specs=WHOLE,
        scratch_shapes=[pltpu.VMEM((lines, LANES), jnp.float32)],
        compiler_params=PARAMS,
        cost_estimate=pl.CostEstimate(flops=4 * rows * width * panel, bytes_accessed=4 * 2**20, transcendentals=0),
        name="pre_dot",
    )(in_vmem(own), in_vmem(other), in_vmem(weights))


def sum_kernel(x_ref, o_ref):
    step = 96
    for b in range(0, o_ref.shape[0], step):
        total = x_ref[0, b : b + step, :].astype(jnp.float32)
        for p in range(1, x_ref.shape[0]):
            total += x_ref[p, b : b + step, :].astype(jnp.float32)
        o_ref[b : b + step, :] = total.astype(o_ref.dtype)


def sum_parts(parts):
    return pl.pallas_call(
        sum_kernel,
        out_shape=pltpu.VMEM(parts.shape[1:], jnp.bfloat16),
        in_specs=[WHOLE],
        out_specs=WHOLE,
        compiler_params=PARAMS,
        cost_estimate=pl.CostEstimate(flops=parts.size, bytes_accessed=2 * parts.size, transcendentals=0),
        name="sum_parts",
    )(in_vmem(parts))


def post_kernel(half_ref, g_ref, w_ref, rows_ref, part_ref, s_ref):
    rows, width = rows_ref.shape
    lines = width // LANES
    s_ref[...] = g_ref[...].reshape(s_ref.shape).astype(jnp.float32)
    for j in range(lines):
        rows_ref[:, j * LANES : (j + 1) * LANES] = s_ref[pl.ds(j, rows, stride=lines), :].astype(rows_ref.dtype)
    for k, place in enumerate((half_ref[2], 1 - half_ref[2])):
        part_ref[place] = lax.dot_general(
            w_ref[k], rows_ref[...], (((1,), (1,)), ((), ())), preferred_element_type=jnp.float32
        ).astype(part_ref.dtype)


def post_dot(half, gathered, weights):
    _, panel, width = weights.shape
    rows = gathered.size // width
    return pl.pallas_call(
        post_kernel,
        out_shape=(pltpu.VMEM((rows, width), jnp.bfloat16), jax.ShapeDtypeStruct((N_HALF, panel, rows), jnp.bfloat16)),
        in_specs=[SCALAR, WHOLE, WHOLE],
        out_specs=(WHOLE, WHOLE),
        scratch_shapes=[pltpu.VMEM((gathered.size // LANES, LANES), jnp.float32)],
        compiler_params=PARAMS,
        cost_estimate=pl.CostEstimate(flops=4 * rows * width * panel, bytes_accessed=6 * 2**20, transcendentals=0),
        name="post_dot",
    )(half, in_vmem(gathered), in_vmem(weights))


def join_kernel(half_ref, w_ref, act_ref, bias_ref, back_ref, w_out, act_out, bias_out):
    panel, width = w_ref.shape
    rows = act_ref.shape[0]
    mine = pl.ds(pl.multiple_of(half_ref[0] * width, LANES), width)
    theirs = pl.ds(pl.multiple_of((1 - half_ref[0]) * width, LANES), width)
    w_out[:, mine] = w_ref[...]
    w_out[:, theirs] = back_ref[:panel, :]
    tail = back_ref[panel:, :].astype(jnp.float32)
    act_out[:, mine] = act_ref[...]
    act_out[:, theirs] = tail[:rows].astype(act_out.dtype)
    bias_out[:, mine] = bias_ref[...]
    bias_out[:, theirs] = tail[rows : rows + 1] + tail[rows + 1 : rows + 2] + tail[rows + 2 : rows + 3]


def join_halves(half, weight_own, act_own, bias_own, back):
    panel, width = weight_own.shape
    hidden, rows = N_HALF * width, act_own.shape[0]
    return pl.pallas_call(
        join_kernel,
        out_shape=(
            jax.ShapeDtypeStruct((panel, hidden), jnp.bfloat16),
            jax.ShapeDtypeStruct((rows, hidden), jnp.bfloat16),
            jax.ShapeDtypeStruct((1, hidden), jnp.float32),
        ),
        in_specs=[SCALAR, WHOLE, WHOLE, WHOLE, WHOLE],
        out_specs=(WHOLE, WHOLE, WHOLE),
        compiler_params=PARAMS,
        cost_estimate=pl.CostEstimate(flops=2**20, bytes_accessed=3 * 2**20, transcendentals=0),
        name="join_halves",
    )(half, weight_own, act_own, bias_own, back)


def interleave_kernel(slim, x_ref, o_ref, s_ref):
    groups, lines = x_ref.shape[0], x_ref.shape[1]
    rows = o_ref.shape[0]
    step = lines // rows
    s_ref[...] = x_ref[...].astype(jnp.float32)
    values = [
        jnp.concatenate([s_ref[c, pl.ds(m, rows, stride=step), :] for m in range(step)], 1) for c in range(groups)
    ]
    for r in range(0, N_ROW, 2):
        pieces = [values[c][:, q * slim : (q + 1) * slim] for q in (r, r + 1) for c in range(groups)]
        width = len(pieces) * slim
        o_ref[:, r // 2 * width : (r // 2 + 1) * width] = jnp.concatenate(pieces, 1).astype(o_ref.dtype)


def interleave(parts, rows, slim):
    groups, lines, _ = parts.shape
    return pl.pallas_call(
        functools.partial(interleave_kernel, slim),
        out_shape=jax.ShapeDtypeStruct((rows, groups * lines // rows * LANES), jnp.bfloat16),
        in_specs=[WHOLE],
        out_specs=WHOLE,
        scratch_shapes=[pltpu.VMEM((groups, lines, LANES), jnp.float32)],
        compiler_params=PARAMS,
        cost_estimate=pl.CostEstimate(flops=2**20, bytes_accessed=2**19, transcendentals=0),
        name="interleave",
    )(parts)


def per_device(tokens, weight, bias, grad_out):
    rows, features = tokens.shape
    panel, hidden = weight.shape
    all_rows = rows * N_ROW
    width = hidden // N_HALF
    f32, bf16 = jnp.float32, jnp.bfloat16
    half = (lax.axis_index("row") // N_YZ) % N_HALF
    first = half == 0
    core = lax.axis_index("col") % 2
    crossed = half ^ core
    half_ref = jnp.stack([half, crossed, core]).astype(jnp.int32)

    def columns(value, which):
        return lax.dynamic_slice_in_dim(value, which * width, width, value.ndim - 1)

    def in_order(own, other, axis):
        return jnp.concatenate([jnp.where(first, own, other), jnp.where(first, other, own)], axis)

    with jax.named_scope("weight_in"):
        give = jnp.concatenate([columns(weight, 1 - half), columns(grad_out, 1 - half)], 0)
        got = lax.ppermute(give, "row", PARTNER)
        weights = both_panels(half_ref, weight, got)
    with jax.named_scope("tokens"):
        t = lax.dynamic_index_in_dim(tokens.reshape(rows, N_PAIR, N_HALF, N_YZ * panel), core, 2, False)
        t = t.reshape(rows, N_PAIR * N_YZ, panel).transpose(1, 0, 2).reshape(N_PAIR, 1, N_YZ, 8, -1)
        t = jnp.broadcast_to(t, (N_PAIR, N_HALF) + t.shape[2:]).reshape(N_ROW, 8, -1)
        t = swap(t, BOTH, ROW_GROUPS)
        t = t.reshape(N_PAIR, N_HALF, N_YZ, rows, panel).transpose(0, 2, 1, 3, 4)
        fetched = t.reshape(all_rows, panel)
        swapped = lax.ppermute(fetched, "col", CORES)
    with jax.named_scope("pre_dot"):
        pair_rows = N_HALF * rows
        bias_half = columns(bias, half).reshape(1, -1, LANES)
        bias_rows = jnp.broadcast_to(bias_half, (pair_rows,) + bias_half.shape[1:]).reshape(-1, LANES)
        upstream = in_order(columns(grad_out, half), got[panel:], 0).reshape(-1, LANES)
        fetched, swapped, bias_rows, upstream = lax.optimization_barrier((fetched, swapped, bias_rows, upstream))
        partial = pre_dot(fetched, swapped, weights)
    with jax.named_scope("pre_xy"):
        partial = swap(partial, "row", PY_GROUPS)
        partial = sum_parts(partial)
    with jax.named_scope("pre_z"):
        partial = swap(partial.reshape(N_Z, -1, LANES), "row", Z_GROUPS)
        pre_act = jnp.sum(partial.astype(f32), axis=0)
    with jax.named_scope("gelu"):
        pre_act = pre_act + bias_rows
        output_value, derivative = gelu_parts(pre_act)
        activation = output_value.astype(bf16)
        grad_pre = (upstream.astype(f32) * derivative).astype(bf16)
        activation, grad_pre = lax.optimization_barrier((activation, grad_pre))
    with jax.named_scope("grad_z"):
        g = swap(jnp.broadcast_to(grad_pre[None], (N_Z,) + grad_pre.shape), "row", Z_GROUPS)
    with jax.named_scope("grad_xy"):
        g = g.reshape(-1, LANES)
        g = swap(jnp.broadcast_to(g[None], (N_PY,) + g.shape), "row", PY_GROUPS)
        g, activation = lax.optimization_barrier((g, activation))
        activation = activation.reshape(N_HALF, rows, width)
    with jax.named_scope("input_dot"):
        g, part = post_dot(half_ref, g, weights)
    with jax.named_scope("weight_dot"):
        over_rows = (((0,), (0,)), ((), ()))
        weight_a = lax.dot_general(fetched, g, over_rows, preferred_element_type=f32).astype(bf16)
        weight_b = lax.dot_general(swapped, g, over_rows, preferred_element_type=f32).astype(bf16)
        weight_own = jnp.where(crossed == 0, weight_a, weight_b)
        weight_other = jnp.where(crossed == 0, weight_b, weight_a)
    with jax.named_scope("bias_sum"):
        bias_half = jnp.sum(g.astype(f32), axis=0)
        high = lax.reduce_precision(bias_half, 8, 7)
        middle = lax.reduce_precision(bias_half - high, 8, 7)
        low = bias_half - high - middle
        pieces = jnp.stack([high, middle, low] + [jnp.zeros_like(low)] * (TAIL - rows - 3)).astype(bf16)
    with jax.named_scope("input_col"):
        slim = panel // N_COL
        part = swap(part.reshape(N_HALF * N_COL, slim, all_rows), BOTH, PAIR_COL_GROUPS)
        part = jnp.sum(part.astype(f32), axis=0).astype(bf16)
    with jax.named_scope("weight_out"):
        give = jnp.concatenate([weight_other, lax.dynamic_index_in_dim(activation, 1 - half, 0, False), pieces], 0)
        part, give = lax.optimization_barrier((part, give))
        back = lax.ppermute(give, "row", PARTNER)
    with jax.named_scope("input_row"):
        part = part.reshape(slim, N_PAIR, N_YZ, N_HALF, rows).transpose(1, 3, 2, 4, 0).reshape(N_ROW, rows * slim)
        part = swap(part, BOTH, ROW_GROUPS)
    with jax.named_scope("input_back"):
        part = part.reshape(N_ROW, rows, slim).transpose(1, 0, 2).reshape(-1, LANES)
        part = swap(jnp.broadcast_to(part[None], (N_COL,) + part.shape), BOTH, COL_GROUPS)
        act_own = lax.dynamic_index_in_dim(activation, half, 0, False)
        outs = join_halves(half_ref, weight_own, act_own, bias_half.reshape(1, -1), back)
        part, weight_grad, activation, bias_grad = lax.optimization_barrier((part,) + tuple(outs))
        bias_grad = bias_grad.reshape(hidden)
        input_grad = interleave(part, rows, slim)
    return (activation, input_grad, weight_grad, bias_grad)


def solution(mesh):
    placed = (P("row", None), P("row", "col"), P("col"), P("row", "col"))
    return jax.shard_map(
        per_device,
        mesh=mesh,
        in_specs=placed,
        out_specs=(P("row", "col"), P("row", None), P("row", "col"), P("col")),
        check_vma=False,
    )
```

```python
import functools
import math

import jax
import jax.numpy as jnp
from jax import lax
from jax.experimental import pallas as pl
from jax.experimental.pallas import tpu as pltpu
from jax.sharding import PartitionSpec as P

root_coeff = math.sqrt(2.0 / math.pi)
cubic_coeff = 0.044715

N_PAIR, N_HALF, N_YZ, N_Z, N_COL, N_ROW = 2, 2, 16, 4, 8, 64
N_PY = 8
LANES = 128
TAIL = 16
BOTH = ("row", "col")


def row_of(pair, half, yz):
    return (pair * N_HALF + half) * N_YZ + yz


def turned(row, chunk):
    low, core = divmod(chunk, 2)
    return row * N_COL + ((low + row) % 4) * 2 + core


ROW_GROUPS = [[turned(r, j) for r in range(N_ROW)] for j in range(N_COL)]
COL_GROUPS = [[turned(r, j) for j in range(N_COL)] for r in range(N_ROW)]
PAIR_COL_GROUPS = [
    [turned(row_of(p, i, yz), j) for i in range(N_HALF) for j in range(N_COL)] for p in range(N_PAIR) for yz in range(N_YZ)
]
PY_GROUPS = [
    [row_of(p, i, y * N_Z + z) for p in range(N_PAIR) for y in range(N_YZ // N_Z)] for i in range(N_HALF) for z in range(N_Z)
]
Z_GROUPS = [[q * N_Z + z for z in range(N_Z)] for q in range(N_ROW // N_Z)]
PARTNER = [(r, r ^ N_YZ) for r in range(N_ROW)]


def gelu_parts(pre_act):
    argument = root_coeff * (pre_act + cubic_coeff * pre_act * pre_act * pre_act)
    tangent = jnp.tanh(argument)
    output_value = 0.5 * pre_act * (1.0 + tangent)
    derivative = 0.5 * (1.0 + tangent) + 0.5 * pre_act * (1.0 - tangent * tangent) * root_coeff * (
        1.0 + 3.0 * cubic_coeff * pre_act * pre_act
    )
    return (output_value, derivative)


def swap(block, axis, groups):
    return lax.all_to_all(block, axis, 0, 0, axis_index_groups=groups)


def in_vmem(value):
    return pltpu.with_memory_space_constraint(value, pltpu.VMEM)


WHOLE = pl.BlockSpec(memory_space=pltpu.VMEM)
SCALAR = pl.BlockSpec(memory_space=pltpu.SMEM)
PARAMS = pltpu.CompilerParams(vmem_limit_bytes=24 * 2**20)


def weight_kernel(half_ref, w_ref, got_ref, o_ref):
    panel, width = o_ref.shape[1:]
    o_ref[0] = w_ref[:, pl.ds(pl.multiple_of(half_ref[0] * width, LANES), width)]
    o_ref[1] = got_ref[:panel, :]


def both_panels(half, weight, got):
    panel, width = weight.shape[0], got.shape[1]
    return pl.pallas_call(
        weight_kernel,
        out_shape=pltpu.VMEM((N_HALF, panel, width), jnp.bfloat16),
        in_specs=[SCALAR, WHOLE, WHOLE],
        out_specs=WHOLE,
        compiler_params=PARAMS,
        cost_estimate=pl.CostEstimate(flops=0, bytes_accessed=3 * 2**20, transcendentals=0),
        name="both_panels",
    )(half, weight, got)


def pre_kernel(own_ref, other_ref, w_ref, o_ref, s_ref):
    rows = own_ref.shape[0]
    lines = w_ref.shape[2] // LANES
    for j in range(0, lines, 2):
        columns = slice(j * LANES, (j + 2) * LANES)
        both = jnp.dot(own_ref[...], w_ref[0, :, columns], preferred_element_type=jnp.float32)
        both += jnp.dot(other_ref[...], w_ref[1, :, columns], preferred_element_type=jnp.float32)
        s_ref[pl.ds(j, rows, stride=lines), :] = both[:, :LANES]
        s_ref[pl.ds(j + 1, rows, stride=lines), :] = both[:, LANES:]
    o_ref[...] = s_ref[...].astype(o_ref.dtype).reshape(o_ref.shape)


def pre_dot(own, other, weights):
    rows, (_, panel, width) = own.shape[0], weights.shape
    lines = rows * width // LANES
    return pl.pallas_call(
        pre_kernel,
        out_shape=pltpu.VMEM((N_PY, lines // N_PY, LANES), jnp.bfloat16),
        in_specs=[WHOLE, WHOLE, WHOLE],
        out_specs=WHOLE,
        scratch_shapes=[pltpu.VMEM((lines, LANES), jnp.float32)],
        compiler_params=PARAMS,
        cost_estimate=pl.CostEstimate(flops=4 * rows * width * panel, bytes_accessed=4 * 2**20, transcendentals=0),
        name="pre_dot",
    )(in_vmem(own), in_vmem(other), in_vmem(weights))


def sum_kernel(x_ref, o_ref):
    step = 96
    for b in range(0, o_ref.shape[0], step):
        total = x_ref[0, b : b + step, :].astype(jnp.float32)
        for p in range(1, x_ref.shape[0]):
            total += x_ref[p, b : b + step, :].astype(jnp.float32)
        o_ref[b : b + step, :] = total.astype(o_ref.dtype)


def sum_parts(parts):
    return pl.pallas_call(
        sum_kernel,
        out_shape=pltpu.VMEM(parts.shape[1:], jnp.bfloat16),
        in_specs=[WHOLE],
        out_specs=WHOLE,
        compiler_params=PARAMS,
        cost_estimate=pl.CostEstimate(flops=parts.size, bytes_accessed=2 * parts.size, transcendentals=0),
        name="sum_parts",
    )(in_vmem(parts))


def post_kernel(half_ref, g_ref, w_ref, rows_ref, part_ref, s_ref):
    rows, width = rows_ref.shape
    lines = width // LANES
    s_ref[...] = g_ref[...].reshape(s_ref.shape).astype(jnp.float32)
    for j in range(lines):
        rows_ref[:, j * LANES : (j + 1) * LANES] = s_ref[pl.ds(j, rows, stride=lines), :].astype(rows_ref.dtype)
    for k, place in enumerate((half_ref[0], 1 - half_ref[0])):
        part_ref[place] = lax.dot_general(
            w_ref[k], rows_ref[...], (((1,), (1,)), ((), ())), preferred_element_type=jnp.float32
        ).astype(part_ref.dtype)


def post_dot(half, gathered, weights):
    _, panel, width = weights.shape
    rows = gathered.size // width
    return pl.pallas_call(
        post_kernel,
        out_shape=(pltpu.VMEM((rows, width), jnp.bfloat16), jax.ShapeDtypeStruct((N_HALF, panel, rows), jnp.bfloat16)),
        in_specs=[SCALAR, WHOLE, WHOLE],
        out_specs=(WHOLE, WHOLE),
        scratch_shapes=[pltpu.VMEM((gathered.size // LANES, LANES), jnp.float32)],
        compiler_params=PARAMS,
        cost_estimate=pl.CostEstimate(flops=4 * rows * width * panel, bytes_accessed=6 * 2**20, transcendentals=0),
        name="post_dot",
    )(half, in_vmem(gathered), in_vmem(weights))


def join_kernel(half_ref, w_ref, act_ref, bias_ref, back_ref, w_out, act_out, bias_out):
    panel, width = w_ref.shape
    rows = act_ref.shape[0]
    mine = pl.ds(pl.multiple_of(half_ref[0] * width, LANES), width)
    theirs = pl.ds(pl.multiple_of((1 - half_ref[0]) * width, LANES), width)
    w_out[:, mine] = w_ref[...]
    w_out[:, theirs] = back_ref[:panel, :]
    tail = back_ref[panel:, :].astype(jnp.float32)
    act_out[:, mine] = act_ref[...]
    act_out[:, theirs] = tail[:rows].astype(act_out.dtype)
    bias_out[:, mine] = bias_ref[...]
    bias_out[:, theirs] = tail[rows : rows + 1] + tail[rows + 1 : rows + 2] + tail[rows + 2 : rows + 3]


def join_halves(half, weight_own, act_own, bias_own, back):
    panel, width = weight_own.shape
    hidden, rows = N_HALF * width, act_own.shape[0]
    return pl.pallas_call(
        join_kernel,
        out_shape=(
            jax.ShapeDtypeStruct((panel, hidden), jnp.bfloat16),
            jax.ShapeDtypeStruct((rows, hidden), jnp.bfloat16),
            jax.ShapeDtypeStruct((1, hidden), jnp.float32),
        ),
        in_specs=[SCALAR, WHOLE, WHOLE, WHOLE, WHOLE],
        out_specs=(WHOLE, WHOLE, WHOLE),
        compiler_params=PARAMS,
        cost_estimate=pl.CostEstimate(flops=2**20, bytes_accessed=3 * 2**20, transcendentals=0),
        name="join_halves",
    )(half, weight_own, act_own, bias_own, back)


def interleave_kernel(slim, x_ref, o_ref, s_ref):
    groups, lines = x_ref.shape[0], x_ref.shape[1]
    rows = o_ref.shape[0]
    step = lines // rows
    s_ref[...] = x_ref[...].astype(jnp.float32)
    values = [
        jnp.concatenate([s_ref[c, pl.ds(m, rows, stride=step), :] for m in range(step)], 1) for c in range(groups)
    ]
    for r in range(0, N_ROW, 2):
        pieces = [values[c][:, q * slim : (q + 1) * slim] for q in (r, r + 1) for c in range(groups)]
        width = len(pieces) * slim
        o_ref[:, r // 2 * width : (r // 2 + 1) * width] = jnp.concatenate(pieces, 1).astype(o_ref.dtype)


def interleave(parts, rows, slim):
    groups, lines, _ = parts.shape
    return pl.pallas_call(
        functools.partial(interleave_kernel, slim),
        out_shape=jax.ShapeDtypeStruct((rows, groups * lines // rows * LANES), jnp.bfloat16),
        in_specs=[WHOLE],
        out_specs=WHOLE,
        scratch_shapes=[pltpu.VMEM((groups, lines, LANES), jnp.float32)],
        compiler_params=PARAMS,
        cost_estimate=pl.CostEstimate(flops=2**20, bytes_accessed=2**19, transcendentals=0),
        name="interleave",
    )(parts)


def per_device(tokens, weight, bias, grad_out):
    rows, features = tokens.shape
    panel, hidden = weight.shape
    all_rows = rows * N_ROW
    width = hidden // N_HALF
    f32, bf16 = jnp.float32, jnp.bfloat16
    half = (lax.axis_index("row") // N_YZ) % N_HALF
    first = half == 0
    half_ref = half.reshape(1).astype(jnp.int32)

    def columns(value, which):
        return lax.dynamic_slice_in_dim(value, which * width, width, value.ndim - 1)

    def in_order(own, other, axis):
        return jnp.concatenate([jnp.where(first, own, other), jnp.where(first, other, own)], axis)

    with jax.named_scope("weight_in"):
        give = jnp.concatenate([columns(weight, 1 - half), columns(grad_out, 1 - half)], 0)
        got = lax.ppermute(give, "row", PARTNER)
        weights = both_panels(half_ref, weight, got)
    with jax.named_scope("tokens"):
        t = tokens.reshape(rows, N_ROW, panel).transpose(1, 0, 2).reshape(N_ROW, 8, -1)
        flipped = t.reshape(N_PAIR, N_HALF, N_YZ, 8, -1)[:, ::-1].reshape(t.shape)
        t = swap(jnp.concatenate([t, flipped], 1), BOTH, ROW_GROUPS)

        def token_rows(value):
            value = value.reshape(N_PAIR, N_HALF, N_YZ, rows, panel).transpose(0, 2, 1, 3, 4)
            return value.reshape(all_rows, panel)

        own, other = token_rows(t[:, :8]), token_rows(t[:, 8:])
    with jax.named_scope("pre_dot"):
        pair_rows = N_HALF * rows
        bias_half = columns(bias, half).reshape(1, -1, LANES)
        bias_rows = jnp.broadcast_to(bias_half, (pair_rows,) + bias_half.shape[1:]).reshape(-1, LANES)
        upstream = in_order(columns(grad_out, half), got[panel:], 0).reshape(-1, LANES)
        own, other, bias_rows, upstream = lax.optimization_barrier((own, other, bias_rows, upstream))
        partial = pre_dot(own, other, weights)
    with jax.named_scope("pre_xy"):
        partial = swap(partial, "row", PY_GROUPS)
        partial = sum_parts(partial)
    with jax.named_scope("pre_z"):
        partial = swap(partial.reshape(N_Z, -1, LANES), "row", Z_GROUPS)
        pre_act = jnp.sum(partial.astype(f32), axis=0)
    with jax.named_scope("gelu"):
        pre_act = pre_act + bias_rows
        output_value, derivative = gelu_parts(pre_act)
        activation = output_value.astype(bf16)
        grad_pre = (upstream.astype(f32) * derivative).astype(bf16)
        activation, grad_pre = lax.optimization_barrier((activation, grad_pre))
    with jax.named_scope("grad_z"):
        g = swap(jnp.broadcast_to(grad_pre[None], (N_Z,) + grad_pre.shape), "row", Z_GROUPS)
    with jax.named_scope("grad_xy"):
        g = g.reshape(-1, LANES)
        g = swap(jnp.broadcast_to(g[None], (N_PY,) + g.shape), "row", PY_GROUPS)
        g, activation = lax.optimization_barrier((g, activation))
        activation = activation.reshape(N_HALF, rows, width)
    with jax.named_scope("input_dot"):
        g, part = post_dot(half_ref, g, weights)
    with jax.named_scope("weight_dot"):
        over_rows = (((0,), (0,)), ((), ()))
        weight_own = lax.dot_general(own, g, over_rows, preferred_element_type=f32).astype(bf16)
        weight_other = lax.dot_general(other, g, over_rows, preferred_element_type=f32).astype(bf16)
    with jax.named_scope("bias_sum"):
        bias_half = jnp.sum(g.astype(f32), axis=0)
        high = lax.reduce_precision(bias_half, 8, 7)
        middle = lax.reduce_precision(bias_half - high, 8, 7)
        low = bias_half - high - middle
        pieces = jnp.stack([high, middle, low] + [jnp.zeros_like(low)] * (TAIL - rows - 3)).astype(bf16)
    with jax.named_scope("weight_out"):
        give = jnp.concatenate([weight_other, lax.dynamic_index_in_dim(activation, 1 - half, 0, False), pieces], 0)
        part, give = lax.optimization_barrier((part, give))
        back = lax.ppermute(give, "row", PARTNER)
    with jax.named_scope("input_col"):
        slim = panel // N_COL
        part = swap(part.reshape(N_HALF * N_COL, slim, all_rows), BOTH, PAIR_COL_GROUPS)
        part = jnp.sum(part.astype(f32), axis=0).astype(bf16)
    with jax.named_scope("input_row"):
        part = part.reshape(slim, N_PAIR, N_YZ, N_HALF, rows).transpose(1, 3, 2, 4, 0).reshape(N_ROW, rows * slim)
        part = swap(part, BOTH, ROW_GROUPS)
    with jax.named_scope("input_back"):
        part = part.reshape(N_ROW, rows, slim).transpose(1, 0, 2).reshape(-1, LANES)
        part = swap(jnp.broadcast_to(part[None], (N_COL,) + part.shape), BOTH, COL_GROUPS)
        act_own = lax.dynamic_index_in_dim(activation, half, 0, False)
        outs = join_halves(half_ref, weight_own, act_own, bias_half.reshape(1, -1), back)
        part, weight_grad, activation, bias_grad = lax.optimization_barrier((part,) + tuple(outs))
        bias_grad = bias_grad.reshape(hidden)
        input_grad = interleave(part, rows, slim)
    return (activation, input_grad, weight_grad, bias_grad)


def solution(mesh):
    placed = (P("row", None), P("row", "col"), P("col"), P("row", "col"))
    return jax.shard_map(
        per_device,
        mesh=mesh,
        in_specs=placed,
        out_specs=(P("row", "col"), P("row", None), P("row", "col"), P("col")),
        check_vma=False,
    )
```
